32 devices in a mesh: rxn: 4 (over y, core), col: 8 (over z, x).
Axes of the slice: x: 2, y: 2, z: 4, core: 2. Of those that a mesh axis runs over, the one named last changes fastest.
Arguments:
- basis: bfloat16 [12288, 16384], P('rxn', 'col'), may hold values from -8 to 8, as said below
- lower_slack: float32 [12288], P('rxn'), may hold values from 0.5 to 4
- upper_slack: float32 [12288], P('rxn'), may hold values from 0.5 to 4
Outputs:
- panel_factor: float32 [16384, 256], P(('col', 'rxn'))
The draws below stay inside these ranges and needn't reach their ends.
Inputs may be any that keep to these rules, and one draw needn't show every extreme that they name: `basis`: finite real entries of order one.
All inputs are finite; a program needn't handle non-finite values.
Results may differ from the reference program's by a relative error of at most 0.00045.
Values may be sent and summed in bfloat16 or wider, within the bound.
No kernel may reach another device: no remote copies, remote signals or barrier semaphores. Data moves between devices by JAX's collectives and lax.ppermute only.
A program may use at most 64 MiB of HBM per device.

```python
import math
import jax
import jax.numpy as jnp
from jax import lax

PANEL = 256
REACTIONS = 12288
COLUMNS = 16384


def draw_basis(key, part):
    key = jax.random.fold_in(key, 11)
    keys = jax.random.split(key, 5)
    noise = jax.random.normal(keys[0], (REACTIONS, COLUMNS), jnp.float32)
    first_rows = jax.random.normal(keys[1], (REACTIONS, 1), jnp.float32)
    second_rows = jax.random.normal(keys[2], (REACTIONS, 1), jnp.float32)
    first_cols = 0.7 * jax.random.normal(keys[3], (1, COLUMNS), jnp.float32)
    second_cols = 0.7 * jax.random.normal(keys[4], (1, COLUMNS), jnp.float32)
    values = noise + first_rows * first_cols + second_rows * second_cols
    return jnp.clip(values, -8.0, 8.0).astype(jnp.bfloat16)


def steps_of(own_key, shape, cuts, smallest, high):
    factor_of = 1.0
    for dim, parts in cuts:
        draws = jax.random.uniform(jax.random.fold_in(jax.random.fold_in(own_key, 6), dim), (parts,), jnp.float32, smallest / len(cuts), high / len(cuts))
        factor_of = factor_of * jnp.repeat(jnp.exp(draws), shape[dim] // parts).reshape((-1,) + (1,) * (len(shape) - 1 - dim))
    return factor_of


def setup_inputs(seed: int = 0) -> dict:
    streams_of = jax.random.split(jax.random.key(seed), 4)
    return {
        "basis": draw_basis(jax.random.fold_in(streams_of[3], 71), 0),
        "lower_slack": jnp.clip(jnp.exp(math.log(4.0) - 2.0794415 * jax.random.uniform(streams_of[1], (REACTIONS,), jnp.float32) ** steps_of(streams_of[1], (REACTIONS,), ((0, 4),), -0.2, 0.2)), 0.5, 4.0),
        "upper_slack": jnp.clip(jnp.exp(math.log(4.0) - 2.0794415 * jax.random.uniform(streams_of[2], (REACTIONS,), jnp.float32) ** steps_of(streams_of[2], (REACTIONS,), ((0, 4),), -0.2, 0.2)), 0.5, 4.0),
    }


def reference(basis, lower_slack, upper_slack):
    weight = 1.0 / (lower_slack * lower_slack) + 1.0 / (upper_slack * upper_slack)
    scaled = weight / jnp.float32(REACTIONS)
    weighted = (basis[:, :PANEL].astype(jnp.float32) * scaled[:, None]).astype(jnp.bfloat16)
    gram = lax.dot_general(basis.astype(jnp.float32), weighted.astype(jnp.float32), (((0,), (0,)), ((), ())), preferred_element_type=jnp.float32)
    factor = jnp.linalg.cholesky(gram[:PANEL, :])
    identity = jnp.eye(PANEL, dtype=jnp.float32)
    inverse = lax.linalg.triangular_solve(factor, identity, left_side=True, lower=True)
    return jnp.dot(gram, inverse.T, precision=lax.Precision.HIGHEST)
```

```python
import functools

import jax
import jax.numpy as jnp
from jax import lax
from jax.experimental import pallas as pl
from jax.experimental.pallas import tpu as pltpu
from jax.sharding import PartitionSpec as P

PANEL = 256
HALF = PANEL // 2
LANES = 128
BLOCK = 64
STRIP = 8
WIRE_SCALE = 1024.0
COLUMN, CORE, AT, BLOCKS = 0, 1, 2, 3
HIGHEST = lax.Precision.HIGHEST
F32 = jnp.float32
PARAMS = pltpu.CompilerParams(vmem_limit_bytes=16 * 2**20)


def ring_order(columns):
    return list(range(0, columns, 2)) + list(range(columns - 1, 0, -2))


def reverse_bits(value, count):
    out, bit = 0, 1
    while bit < count:
        out = out * 2 + (1 if value & bit else 0)
        bit *= 2
    return out


def to_column(value, pairs):
    return lax.ppermute(value, "col", pairs)


def swap(value, bit):
    size = lax.axis_size("rxn")
    return lax.ppermute(value, "rxn", [(i, i ^ bit) for i in range(size)])


def prepare_kernel(total, count, where_ref, panel_ref, lower_ref, upper_ref, *refs):
    pieces, (keep_ref, send_ref, diag_ref) = refs[:count], refs[count:]
    depth = pieces[0].shape[1]
    low, up = lower_ref[...], upper_ref[...]
    scaled = (1.0 / (low * low) + 1.0 / (up * up)) / total
    diag = jnp.zeros((PANEL, PANEL), F32)
    for line in range(scaled.shape[0]):
        panel = panel_ref[line * LANES : (line + 1) * LANES, :]
        weighted = (panel.astype(F32).T * scaled[line : line + 1, :]).astype(jnp.bfloat16)
        diag += jnp.dot(weighted, panel, preferred_element_type=F32)
        start = line * LANES
        while start < (line + 1) * LANES:
            piece, inside = divmod(start, depth)
            end = min((line + 1) * LANES, (piece + 1) * depth)
            part = weighted[:, start - line * LANES : end - line * LANES]
            if piece == 0:
                part = jnp.where(where_ref[COLUMN] == 0, part.astype(F32), 0.0).astype(jnp.bfloat16)
            pieces[piece][:, inside : inside + end - start] = part
            start = end
    diag_ref[...] = diag
    core = where_ref[CORE]
    keep_ref[...] = diag_ref[pl.ds(pl.multiple_of(core * HALF, HALF), HALF), :]
    send_ref[...] = diag_ref[pl.ds(pl.multiple_of((1 - core) * HALF, HALF), HALF), :]


def prepare(place, basis, lower, upper, total, count):
    rows = basis.shape[0]
    depth = rows // count
    piece = jax.ShapeDtypeStruct((PANEL, depth), jnp.bfloat16)
    half = jax.ShapeDtypeStruct((HALF, PANEL), F32)
    whole = lambda *shape: pl.BlockSpec(shape, lambda i, s: (0, 0))
    lines = rows // LANES
    slacks = [x.reshape(lines, LANES) for x in (lower, upper)]
    return pl.pallas_call(
        functools.partial(prepare_kernel, float(total), count),
        out_shape=[piece] * count + [half, half],
        grid_spec=pltpu.PrefetchScalarGridSpec(
            num_scalar_prefetch=1,
            grid=(1,),
            in_specs=[whole(rows, PANEL), whole(lines, LANES), whole(lines, LANES)],
            out_specs=[whole(PANEL, depth)] * count + [whole(HALF, PANEL)] * 2,
            scratch_shapes=[pltpu.VMEM((PANEL, PANEL), F32)],
        ),
        compiler_params=PARAMS,
        name="prepare",
    )(place, *[pltpu.with_memory_space_constraint(x, pltpu.HBM) for x in (basis, *slacks)])


def eliminate(work):
    done, width = [], work.shape[1]
    for start in range(0, work.shape[0], STRIP):
        rows = work.shape[0]
        row = lax.broadcasted_iota(jnp.int32, (rows, width), 0)
        column = [jnp.broadcast_to(work[:, start + j : start + j + 1], (rows, width)) for j in range(STRIP)]
        for k in range(STRIP):
            root = lax.rsqrt(column[k][k : k + 1, :])
            pivot_row = work[k : k + 1, :] * root
            below = jnp.where(row > k, column[k] * root, 0.0)
            work = jnp.where(row == k, pivot_row, work - below * pivot_row)
            for j in range(k + 1, STRIP):
                column[j] = column[j] - below * (column[j][k : k + 1, :] * root)
        done.append(work[:STRIP])
        work = work[STRIP:]
    return jnp.concatenate(done, 0)


def invert_kernel(where_ref, mine_ref, other_ref, out_ref, work):
    out_ref[...] = jnp.zeros_like(out_ref)

    @pl.when(where_ref[COLUMN] == 0)
    def _():
        invert_diagonal(where_ref[CORE], mine_ref, other_ref, out_ref, work)


def invert_diagonal(core, mine_ref, other_ref, out_ref, work):
    mine = pl.ds(pl.multiple_of(core * HALF, HALF), HALF)
    other = pl.ds(pl.multiple_of((1 - core) * HALF, HALF), HALF)
    work[mine, :PANEL] = mine_ref[...]
    work[other, :PANEL] = other_ref[...]
    row = lax.broadcasted_iota(jnp.int32, (PANEL, PANEL), 0)
    col = lax.broadcasted_iota(jnp.int32, (PANEL, PANEL), 1)
    work[:, PANEL:] = jnp.where(row == col, 1.0, 0.0).astype(F32)
    row = lax.broadcasted_iota(jnp.int32, (BLOCK, 128), 0)
    col = lax.broadcasted_iota(jnp.int32, (BLOCK, 128), 1)
    for low in range(0, PANEL, BLOCK):
        base = low // 128 * 128
        square = work[low : low + BLOCK, base : base + 128]
        if low > base:
            square = pltpu.roll(square, 128 - (low - base), 1)
        square = jnp.where(col < BLOCK, square, jnp.where(col - BLOCK == row, 1.0, 0.0))
        corner = pltpu.roll(eliminate(square), 128 - BLOCK, 1)[:, :BLOCK]
        end = PANEL + (low + BLOCK + 127) // 128 * 128
        scaled = jnp.dot(corner, work[low : low + BLOCK, base:end], precision=HIGHEST, preferred_element_type=F32)
        work[low : low + BLOCK, base:end] = scaled
        rest = low + BLOCK
        if rest < PANEL:
            left = rest // 128 * 128
            update = lax.dot_general(
                scaled[:, left - base : PANEL - base],
                scaled[:, left - base :],
                (((0,), (0,)), ((), ())),
                precision=HIGHEST,
                preferred_element_type=F32,
            )
            work[rest:PANEL, left:end] = work[rest:PANEL, left:end] - update[rest - left :]
    row = lax.broadcasted_iota(jnp.int32, (HALF, PANEL), 0) + core * HALF
    col = lax.broadcasted_iota(jnp.int32, (HALF, PANEL), 1)
    out_ref[...] = jnp.where(row >= col, work[mine, PANEL:], 0.0)


def invert(place, mine, other):
    half = pl.BlockSpec((HALF, PANEL), lambda i, s: (0, 0))
    return pl.pallas_call(
        invert_kernel,
        out_shape=jax.ShapeDtypeStruct((HALF, PANEL), F32),
        grid_spec=pltpu.PrefetchScalarGridSpec(
            num_scalar_prefetch=1,
            grid=(1,),
            in_specs=[half, half],
            out_specs=half,
            scratch_shapes=[pltpu.VMEM((PANEL, 2 * PANEL), F32)],
        ),
        compiler_params=PARAMS,
        cost_estimate=pl.CostEstimate(flops=8 * 10**9, bytes_accessed=2**19, transcendentals=0),
        name="invert",
    )(place, mine, other)


def gram_kernel(count, has_total, where_ref, *refs):
    pieces, tiles, rest = refs[:count], refs[count : 2 * count], refs[2 * count :]
    total = rest[0][0] if has_total else None
    for piece, tile in zip(pieces, tiles):
        term = jnp.dot(piece[...], tile[...], preferred_element_type=F32)
        total = term if total is None else total + term
    rest[-1][0] = total


def add_gram(place, basis, total, pieces, offsets, shares, columns, first, count):
    rows, cols = basis.shape
    depth, share, number = rows // columns, cols // shares, len(pieces)
    tile = lambda offset: pl.BlockSpec(
        (depth, share), lambda j, s: (lax.rem(s[AT] + (offset + columns), columns), s[BLOCKS + first + j])
    )
    piece = pl.BlockSpec((PANEL, depth), lambda j, s: (0, 0))
    in_specs = [piece] * number + [tile(offset) for offset in offsets]
    operands = [*pieces, *([basis] * number)]
    if total is not None:
        in_specs.append(pl.BlockSpec((1, PANEL, share), lambda j, s: (first + j, 0, 0)))
        operands.append(total)
    return pl.pallas_call(
        functools.partial(gram_kernel, number, total is not None),
        out_shape=jax.ShapeDtypeStruct((count, PANEL, share), F32),
        grid_spec=pltpu.PrefetchScalarGridSpec(
            num_scalar_prefetch=1,
            grid=(count,),
            in_specs=in_specs,
            out_specs=pl.BlockSpec((1, PANEL, share), lambda j, s: (j, 0, 0)),
        ),
        compiler_params=PARAMS,
        input_output_aliases={2 * number + 1: 0} if total is not None and count == shares else {},
        cost_estimate=pl.CostEstimate(
            flops=2 * number * depth * PANEL * share * count,
            bytes_accessed=count * (number * depth * share * 2 + 8 * PANEL * share),
            transcendentals=0,
        ),
        name="gram",
    )(place, *operands)


def transform_kernel(where_ref, mine_ref, other_ref, kept_ref, came_ref, out_ref, inverse):
    core = where_ref[CORE]
    inverse[pl.ds(pl.multiple_of(core * HALF, HALF), HALF), :] = mine_ref[...]
    inverse[pl.ds(pl.multiple_of((1 - core) * HALF, HALF), HALF), :] = other_ref[...]
    gram = (kept_ref[0] + came_ref[0]).T
    out_ref[0] = lax.dot_general(
        gram, inverse[...], (((1,), (1,)), ((), ())), precision=HIGHEST, preferred_element_type=F32
    )


def transform(place, mine, other, kept, came):
    count, _, share = kept.shape
    half = pl.BlockSpec((HALF, PANEL), lambda j, s: (0, 0))
    gram = pl.BlockSpec((1, PANEL, share), lambda j, s: (j, 0, 0))
    return pl.pallas_call(
        transform_kernel,
        out_shape=jax.ShapeDtypeStruct((count, share, PANEL), F32),
        grid_spec=pltpu.PrefetchScalarGridSpec(
            num_scalar_prefetch=1,
            grid=(count,),
            in_specs=[half, half, gram, gram],
            out_specs=pl.BlockSpec((1, share, PANEL), lambda j, s: (j, 0, 0)),
            scratch_shapes=[pltpu.VMEM((PANEL, PANEL), F32)],
        ),
        compiler_params=PARAMS,
        name="transform",
    )(place, mine, other, kept, came)


def on_device(basis, lower_slack, upper_slack):
    rows = basis.shape[0]
    shares, columns = lax.axis_size("rxn"), lax.axis_size("col")
    me, column = lax.axis_index("rxn"), lax.axis_index("col")
    order = ring_order(columns)
    relay, middle = order[-1], columns // 2
    at = sum(jnp.where(column == c, p, 0) for p, c in enumerate(order))
    blocks = [me ^ reverse_bits(j, shares) for j in range(shares)]
    place = jnp.stack([column, me % 2, at, *blocks]).astype(jnp.int32)
    *pieces, keep, send = prepare(place, basis, lower_slack, upper_slack, rows * shares, columns)
    basis = pltpu.with_memory_space_constraint(basis, pltpu.VMEM)

    half = keep + swap(send, 1)
    half, *pieces[1:] = lax.optimization_barrier((half, *pieces[1:]))
    bit = 2
    while bit < shares:
        half = half + swap(half, bit)
        bit *= 2

    through = list(range(middle + 1, columns - 1))
    near = list(range(1, middle + 1))
    to_relay = lambda p: to_column(pieces[p], [(0, relay)])
    direct = lambda p: to_column(pieces[p], [(0, order[p])])
    far = [to_relay(p) for p in through]
    parts = [pieces[0]] + [direct(p) for p in near[:-2]]
    late = [*near[-2:], columns - 1]
    half, *moved = lax.optimization_barrier((half, *[pieces[p] for p in late]))
    for p, x in zip(late, moved):
        pieces[p] = x
    other = swap(half, 1)
    parts += [direct(near[-2]), to_relay(columns - 1), direct(near[-1])]
    inverse = invert(place, half, other)
    inverse, *far = lax.optimization_barrier((inverse, *far))
    parts += [to_column(x, [(relay, order[p])]) for x, p in zip(far, through)]
    held = functools.reduce(lambda a, b: a + b, parts)

    forward = [(order[i], order[(i + 1) % columns]) for i in range(columns)]
    backward = [(b, a) for a, b in forward]
    holders, strides = [0], [1] + [columns >> i for i in range(1, columns.bit_length() - 1)]
    gram = lambda total, pending, first, count: add_gram(
        place, basis, total, *zip(*pending), shares, columns, first, count
    )
    pending, total = [(held, 0)], None
    ahead = back = held
    for step in range(1, middle + 1):
        ahead = to_column(ahead, forward)
        came = [(ahead, -step)]
        if step < middle:
            back = to_column(back, backward)
            came.append((back, step))
        if strides:
            stride = strides.pop(0)
            inverse = inverse + to_column(inverse, [(i, i + stride) for i in holders])
            holders += [i + stride for i in holders]
        total, pending = gram(total, pending, 0, shares), came
        if step < middle:
            ahead, back, inverse, total = lax.optimization_barrier((ahead, back, inverse, total))
    inverse_other = swap(inverse, 1)

    quarter = shares // 4
    finish = lambda q: gram(total, pending, q * quarter, quarter)
    came = swap(finish(3), 1)
    away = transform(place, inverse, inverse_other, finish(1), came)
    came = swap(finish(2), 1)
    mine = transform(place, inverse, inverse_other, finish(0), came)
    bit = 2
    while True:
        mine = mine + swap((away * WIRE_SCALE).astype(jnp.float16), bit).astype(F32) * (1.0 / WIRE_SCALE)
        if mine.shape[0] == 1:
            return mine[0]
        half = mine.shape[0] // 2
        mine, away = mine[:half], mine[half:]
        bit *= 2


def solution(mesh):
    return jax.shard_map(
        on_device,
        mesh=mesh,
        in_specs=(P("rxn", "col"), P("rxn"), P("rxn")),
        out_specs=P(("col", "rxn"), None),
        check_vma=False,
    )
```

```python
import functools

import jax
import jax.numpy as jnp
from jax import lax
from jax.experimental import pallas as pl
from jax.experimental.pallas import tpu as pltpu
from jax.sharding import PartitionSpec as P

PANEL = 256
HALF = PANEL // 2
LANES = 128
BLOCK = 64
STRIP = 8
COLUMN, CORE, AT, BLOCKS = 0, 1, 2, 3
SMEM, VMEM, HBM = (pl.BlockSpec(memory_space=space) for space in (pltpu.SMEM, pltpu.VMEM, pltpu.HBM))
HIGHEST = lax.Precision.HIGHEST
F32 = jnp.float32
PARAMS = pltpu.CompilerParams(vmem_limit_bytes=16 * 2**20)


def ring_order(columns):
    return list(range(0, columns, 2)) + list(range(columns - 1, 0, -2))


def reverse_bits(value, count):
    out, bit = 0, 1
    while bit < count:
        out = out * 2 + (1 if value & bit else 0)
        bit *= 2
    return out


def to_column(value, pairs):
    return lax.ppermute(value, "col", pairs)


def swap(value, bit, column=None):
    shares, columns = lax.axis_size("rxn"), lax.axis_size("col")
    on = range(columns) if column is None else [column]
    pairs = [(i * columns + c, (i ^ bit) * columns + c) for i in range(shares) for c in on]
    return lax.ppermute(value, ("rxn", "col"), pairs)


def cut_kernel(place_ref, basis_ref, *refs):
    pieces, sems = refs[:-1], refs[-1]
    pieces[0][...] = jnp.zeros_like(pieces[0])

    @pl.when(place_ref[COLUMN] == 0)
    def _():
        depth = pieces[0].shape[0]
        copies = [
            pltpu.make_async_copy(basis_ref.at[pl.ds(p * depth, depth), pl.ds(0, PANEL)], piece, sems.at[p])
            for p, piece in enumerate(pieces)
        ]
        for copy in copies:
            copy.start()
        for copy in copies:
            copy.wait()


def cut_panel(place, basis, count):
    depth = basis.shape[0] // count
    return pl.pallas_call(
        cut_kernel,
        out_shape=[jax.ShapeDtypeStruct((depth, PANEL), jnp.bfloat16)] * count,
        in_specs=[SMEM, HBM],
        out_specs=[VMEM] * count,
        scratch_shapes=[pltpu.SemaphoreType.DMA((count,))],
        compiler_params=PARAMS,
        name="cut_panel",
    )(place, basis)


def eliminate(work):
    done, width = [], work.shape[1]
    for start in range(0, work.shape[0], STRIP):
        rows = work.shape[0]
        row = lax.broadcasted_iota(jnp.int32, (rows, width), 0)
        column = [jnp.broadcast_to(work[:, start + j : start + j + 1], (rows, width)) for j in range(STRIP)]
        for k in range(STRIP):
            root = lax.rsqrt(column[k][k : k + 1, :])
            pivot_row = work[k : k + 1, :] * root
            below = jnp.where(row > k, column[k] * root, 0.0)
            work = jnp.where(row == k, pivot_row, work - below * pivot_row)
            for j in range(k + 1, STRIP):
                column[j] = column[j] - below * (column[j][k : k + 1, :] * root)
        done.append(work[:STRIP])
        work = work[STRIP:]
    return jnp.concatenate(done, 0)


def invert_kernel(place_ref, mine_ref, other_ref, out_ref, work):
    core = place_ref[CORE]
    mine = pl.ds(pl.multiple_of(core * HALF, HALF), HALF)
    other = pl.ds(pl.multiple_of((1 - core) * HALF, HALF), HALF)
    work[mine, :PANEL] = mine_ref[...]
    work[other, :PANEL] = other_ref[...]
    gram = work[:, :PANEL]
    work[:, :PANEL] = 0.5 * (gram + gram.T)
    row = lax.broadcasted_iota(jnp.int32, (PANEL, PANEL), 0)
    col = lax.broadcasted_iota(jnp.int32, (PANEL, PANEL), 1)
    work[:, PANEL:] = jnp.where(row == col, 1.0, 0.0).astype(F32)
    row = lax.broadcasted_iota(jnp.int32, (BLOCK, 128), 0)
    col = lax.broadcasted_iota(jnp.int32, (BLOCK, 128), 1)
    for low in range(0, PANEL, BLOCK):
        base = low // 128 * 128
        square = work[low : low + BLOCK, base : base + 128]
        if low > base:
            square = pltpu.roll(square, 128 - (low - base), 1)
        square = jnp.where(col < BLOCK, square, jnp.where(col - BLOCK == row, 1.0, 0.0))
        corner = pltpu.roll(eliminate(square), 128 - BLOCK, 1)[:, :BLOCK]
        end = PANEL + (low + BLOCK + 127) // 128 * 128
        scaled = jnp.dot(corner, work[low : low + BLOCK, base:end], precision=HIGHEST, preferred_element_type=F32)
        work[low : low + BLOCK, base:end] = scaled
        rest = low + BLOCK
        if rest < PANEL:
            left = rest // 128 * 128
            update = lax.dot_general(
                scaled[:, left - base : PANEL - base],
                scaled[:, left - base :],
                (((0,), (0,)), ((), ())),
                precision=HIGHEST,
                preferred_element_type=F32,
            )
            work[rest:PANEL, left:end] = work[rest:PANEL, left:end] - update[rest - left :]
    row = lax.broadcasted_iota(jnp.int32, (PANEL, PANEL), 0)
    col = lax.broadcasted_iota(jnp.int32, (PANEL, PANEL), 1)
    out_ref[...] = jnp.where(row >= col, work[:, PANEL:], 0.0)


def invert(place, mine, other):
    return pl.pallas_call(
        invert_kernel,
        out_shape=jax.ShapeDtypeStruct((PANEL, PANEL), F32),
        in_specs=[SMEM, VMEM, VMEM],
        out_specs=VMEM,
        scratch_shapes=[pltpu.VMEM((PANEL, 2 * PANEL), F32)],
        compiler_params=PARAMS,
        cost_estimate=pl.CostEstimate(flops=3*10**9, bytes_accessed=2**19, transcendentals=0),
        name="invert",
    )(place, mine, other)


def weigh(total, at, lower_ref, upper_ref, piece):
    low, up = lower_ref[pl.ds(at, 1), :], upper_ref[pl.ds(at, 1), :]
    scaled = (1.0 / (low * low) + 1.0 / (up * up)) / total
    return (piece.astype(F32).T * scaled).astype(jnp.bfloat16)


def piece_at(place_ref, offset, columns):
    return lax.rem(place_ref[AT] + (offset + columns), columns)


def block_lanes(place_ref, block, share):
    return pl.ds(pl.multiple_of(place_ref[BLOCKS + block] * share, share), share)


def fetches(place_ref, basis_ref, columns, offsets, tiles, sems):
    depth = basis_ref.shape[0] // columns
    copies = []
    for i, (offset, tile) in enumerate(zip(offsets, tiles)):
        rows = pl.ds(pl.multiple_of(piece_at(place_ref, offset, columns) * depth, depth), depth)
        copies.append(pltpu.make_async_copy(basis_ref.at[rows, :], tile, sems.at[i]))
    return copies


def gram_kernel(offsets, later, total, fresh, place_ref, lower_ref, upper_ref, basis_ref, *refs):
    number, columns = len(offsets), lower_ref.shape[0]
    pieces, weighted, sems = refs[:number], refs[-number - 1 : -1], refs[-1]
    if fresh:
        outs, tiles = refs[number : -2 * number - 1], refs[-2 * number - 1 : -number - 1]
    else:
        tiles, adds, outs = refs[number : 2 * number], refs[2 * number :], refs[2 * number + 2 : -number - 1]
    copies = fetches(place_ref, basis_ref, columns, later, outs[2:], sems)
    own = fetches(place_ref, basis_ref, columns, offsets, tiles, sems.at[pl.ds(len(later), number)]) if fresh else []
    for copy in own + copies:
        copy.start()
    diagonal = jnp.zeros((PANEL, PANEL), F32) if fresh else adds[1][...]
    for offset, piece, held in zip(offsets, pieces, weighted):
        at = piece_at(place_ref, offset, columns)
        held[...] = weigh(total, at, lower_ref, upper_ref, piece[...])
        diagonal += jnp.dot(held[...], piece[...], preferred_element_type=F32)
    outs[1][...] = diagonal
    for copy in own:
        copy.wait()
    count, _, share = outs[0].shape

    def block(j, carry):
        lanes = block_lanes(place_ref, j, share)
        gram = jnp.zeros((PANEL, share), F32) if fresh else adds[0][j]
        for held, tile in zip(weighted, tiles):
            gram += jnp.dot(held[...], tile[:, lanes], preferred_element_type=F32)
        outs[0][j] = gram
        return carry

    lax.fori_loop(0, count, block, 0)
    for copy in copies:
        copy.wait()


def add_gram(total, shares, shared, sums, pieces, offsets, tiles, later):
    basis, number, depth = shared[-1], len(pieces), pieces[0].shape[0]
    cols = basis.shape[1]
    share = cols // shares
    tile = (depth, cols)
    base = len(shared) + 2 * number
    return pl.pallas_call(
        functools.partial(gram_kernel, offsets, later, float(total), not sums),
        out_shape=[
            jax.ShapeDtypeStruct((shares, PANEL, share), F32),
            jax.ShapeDtypeStruct((PANEL, PANEL), F32),
            *[jax.ShapeDtypeStruct(tile, jnp.bfloat16)] * len(later),
        ],
        in_specs=[SMEM, VMEM, VMEM, HBM] + [VMEM] * (number + len(tiles) + len(sums)),
        out_specs=[VMEM] * (2 + len(later)),
        scratch_shapes=[pltpu.VMEM(tile, jnp.bfloat16)] * (0 if sums else number)
        + [pltpu.VMEM((PANEL, depth), jnp.bfloat16)] * number
        + [pltpu.SemaphoreType.DMA((number + len(later),))],
        compiler_params=PARAMS,
        input_output_aliases={base: 0, base + 1: 1} if sums else {},
        cost_estimate=pl.CostEstimate(
            flops=2 * number * depth * PANEL * cols,
            bytes_accessed=number * depth * cols * 2 + 8 * PANEL * cols,
            transcendentals=0,
        ),
        name="gram",
    )(*shared, *pieces, *tiles, *sums)


def last_kernel(offset, total, place_ref, lower_ref, upper_ref, tile_ref, top_ref, bottom_ref, *refs):
    gram_ref, diagonal_ref, sent_ref, away_ref, mine_ref, other_ref, weighted_ref, sum_ref = refs
    piece = jnp.concatenate([top_ref[...], bottom_ref[...]], 0)
    at = piece_at(place_ref, offset, lower_ref.shape[0])
    weighted_ref[...] = weigh(total, at, lower_ref, upper_ref, piece)
    sum_ref[...] = diagonal_ref[...] + jnp.dot(weighted_ref[...], piece, preferred_element_type=F32)
    core = place_ref[CORE]
    mine_ref[...] = sum_ref[pl.ds(pl.multiple_of(core * HALF, HALF), HALF), :]
    other_ref[...] = sum_ref[pl.ds(pl.multiple_of((1 - core) * HALF, HALF), HALF), :]
    add_blocks(place_ref, gram_ref, weighted_ref, tile_ref, [(3, sent_ref), (1, away_ref)])


def add_blocks(place_ref, gram_ref, weighted_ref, tile_ref, quarters):
    for number, out_ref in quarters:
        count, _, share = out_ref.shape
        for j in range(count):
            block = number * count + j
            lanes = block_lanes(place_ref, block, share)
            term = jnp.dot(weighted_ref[...], tile_ref[:, lanes], preferred_element_type=F32)
            out_ref[j] = gram_ref[block] + term


def rest_kernel(place_ref, weighted_ref, tile_ref, gram_ref, sent_ref, kept_ref):
    add_blocks(place_ref, gram_ref, weighted_ref, tile_ref, [(2, sent_ref), (0, kept_ref)])


def finish_gram(total, shared, sums, tile, top, bottom, offset):
    place, lower, upper, _ = shared
    gram, diagonal = sums
    shares, _, share = gram.shape
    depth = tile.shape[0]
    quarter = jax.ShapeDtypeStruct((shares // 4, PANEL, share), F32)
    half = jax.ShapeDtypeStruct((HALF, PANEL), F32)
    cost = pl.CostEstimate(flops=depth * PANEL * share * shares, bytes_accessed=2**21, transcendentals=0)
    third, first, mine, other, weighted = pl.pallas_call(
        functools.partial(last_kernel, offset, float(total)),
        out_shape=[quarter, quarter, half, half, jax.ShapeDtypeStruct((PANEL, depth), jnp.bfloat16)],
        in_specs=[SMEM] + [VMEM] * 7,
        out_specs=[VMEM] * 5,
        scratch_shapes=[pltpu.VMEM((PANEL, PANEL), F32)],
        compiler_params=PARAMS,
        cost_estimate=cost,
        name="last",
    )(place, lower, upper, tile, top, bottom, gram, diagonal)
    second, zeroth = pl.pallas_call(
        rest_kernel,
        out_shape=[quarter, quarter],
        in_specs=[SMEM] + [VMEM] * 3,
        out_specs=[VMEM] * 2,
        compiler_params=PARAMS,
        cost_estimate=cost,
        name="rest",
    )(place, weighted, tile, gram)
    return zeroth, first, second, third, mine, other


def transform_kernel(inverse_ref, *refs):
    gram = refs[0][0]
    for ref in refs[1:-1]:
        gram = gram + ref[0]
    refs[-1][...] = lax.dot_general(
        gram.T, inverse_ref[...], (((1,), (1,)), ((), ())), precision=HIGHEST, preferred_element_type=F32
    )


def transform(inverse, terms):
    share = terms[0].shape[2]
    return pl.pallas_call(
        transform_kernel,
        out_shape=jax.ShapeDtypeStruct((share, PANEL), F32),
        in_specs=[VMEM] * (1 + len(terms)),
        out_specs=VMEM,
        compiler_params=PARAMS,
        cost_estimate=pl.CostEstimate(
            flops=12 * share * PANEL * PANEL, bytes_accessed=12 * share * PANEL, transcendentals=0
        ),
        name="transform",
    )(inverse, *terms)


def on_device(basis, lower_slack, upper_slack):
    rows = basis.shape[0]
    shares, columns = lax.axis_size("rxn"), lax.axis_size("col")
    me, column = lax.axis_index("rxn"), lax.axis_index("col")
    order = ring_order(columns)
    relay, middle = order[-1], columns // 2
    at = sum(jnp.where(column == c, p, 0) for p, c in enumerate(order))
    blocks = [me ^ reverse_bits(j, shares) for j in range(shares)]
    place = jnp.stack([column, me % 2, at, *blocks]).astype(jnp.int32)
    basis = pltpu.with_memory_space_constraint(basis, pltpu.HBM)
    pieces = cut_panel(place, basis, columns)
    slacks = [x.reshape(columns, rows // columns) for x in (lower_slack, upper_slack)]
    shared = (place, *slacks, basis)

    through, near = range(middle + 1, columns - 1), range(1, middle + 1)
    to_relay = lambda p: to_column(pieces[p], [(0, relay)])
    parts = [to_column(pieces[p], [(0, order[p])]) for p in near]
    far = [to_relay(p) for p in through]
    parts.append(to_relay(columns - 1))
    parts += [to_column(x, [(relay, order[p])]) for x, p in zip(far, through)]
    held = functools.reduce(lambda a, b: a + b, parts, pieces[0])

    forward = [(order[i], order[(i + 1) % columns]) for i in range(columns)]
    backward = [(b, a) for a, b in forward]
    gram = functools.partial(add_gram, rows * shares, shares, shared)
    pieces, offsets, sums, tiles = [held], [0], [], []
    ahead = back = held
    for step in range(1, middle):
        ahead, back = to_column(ahead, forward), to_column(back, backward)
        later = [-step, step]
        *sums, left, right = gram(sums, pieces, offsets, tiles, later)
        ahead, back, left, right, *sums = lax.optimization_barrier((ahead, back, left, right, *sums))
        pieces, offsets, tiles = [ahead, back], later, [left, right]
    cut = rows // columns // 2
    top, bottom = to_column(ahead[:cut], forward), to_column(back[cut:], backward)
    *sums, tile = gram(sums, pieces, offsets, tiles, [middle])
    zeroth, first, second, third, mine, other = finish_gram(rows * shares, shared, sums, tile, top, bottom, middle)

    mine, third = mine + swap(other, 1), swap(third, 1)
    away, second = first + third, swap(second, 1)
    mine, away = lax.optimization_barrier((mine, away))
    part, came = swap(mine, 2), swap(away, 2)
    mine, bit = mine + part, 4
    while bit < shares:
        mine = mine + swap(mine, bit)
        bit *= 2
    other = swap(mine, 1)
    inverse = invert(place, mine, other)
    terms, bit = [zeroth, second, came], 4
    while bit < shares:
        mine = functools.reduce(lambda a, b: a + b, terms)
        middle = mine.shape[0] // 2
        terms = [mine[:middle], swap(mine[middle:], bit)]
        bit *= 2
    return transform(inverse, terms)


def solution(mesh):
    return jax.shard_map(
        on_device,
        mesh=mesh,
        in_specs=(P("rxn", "col"), P("rxn"), P("rxn")),
        out_specs=P(("col", "rxn"), None),
        check_vma=False,
    )
```

```python
import functools

import jax
import jax.numpy as jnp
from jax import lax
from jax.experimental import pallas as pl
from jax.experimental.pallas import tpu as pltpu
from jax.sharding import PartitionSpec as P

PANEL = 256
HALF = PANEL // 2
LANES = 128
BLOCK = 64
STRIP = 8
COLUMN, CORE, AT, BLOCKS = 0, 1, 2, 3
SMEM, VMEM, HBM = (pl.BlockSpec(memory_space=space) for space in (pltpu.SMEM, pltpu.VMEM, pltpu.HBM))
HIGHEST = lax.Precision.HIGHEST
F32 = jnp.float32
PARAMS = pltpu.CompilerParams(vmem_limit_bytes=16 * 2**20)


def ring_order(columns):
    return list(range(0, columns, 2)) + list(range(columns - 1, 0, -2))


def reverse_bits(value, count):
    out, bit = 0, 1
    while bit < count:
        out = out * 2 + (1 if value & bit else 0)
        bit *= 2
    return out


def to_column(value, pairs):
    return lax.ppermute(value, "col", pairs)


def swap(value, bit, column=None):
    shares, columns = lax.axis_size("rxn"), lax.axis_size("col")
    on = range(columns) if column is None else [column]
    pairs = [(i * columns + c, (i ^ bit) * columns + c) for i in range(shares) for c in on]
    return lax.ppermute(value, ("rxn", "col"), pairs)


def cut_kernel(choices, place_ref, basis_ref, *refs):
    pieces, sems = refs[:-1], refs[-1]
    pieces[0][...] = jnp.zeros_like(pieces[0])

    @pl.when(place_ref[COLUMN] == 0)
    def _():
        depth = pieces[0].shape[0]
        copies = []
        for i, (piece, choice) in enumerate(zip(pieces, choices)):
            row = pl.multiple_of(jnp.where(place_ref[CORE] == 0, choice[0], choice[1]) * depth, depth)
            copies.append(
                pltpu.make_async_copy(basis_ref.at[pl.ds(row, depth), pl.ds(0, PANEL)], piece, sems.at[i])
            )
        for copy in copies:
            copy.start()
        for copy in copies:
            copy.wait()


def cut_panel(place, basis, choices, count):
    depth = basis.shape[0] // count
    return pl.pallas_call(
        functools.partial(cut_kernel, choices),
        out_shape=[jax.ShapeDtypeStruct((depth, PANEL), jnp.bfloat16)] * len(choices),
        in_specs=[SMEM, HBM],
        out_specs=[VMEM] * len(choices),
        scratch_shapes=[pltpu.SemaphoreType.DMA((len(choices),))],
        compiler_params=PARAMS,
        name="cut_panel",
    )(place, basis)


def eliminate(work):
    done, width = [], work.shape[1]
    for start in range(0, work.shape[0], STRIP):
        rows = work.shape[0]
        row = lax.broadcasted_iota(jnp.int32, (rows, width), 0)
        column = [jnp.broadcast_to(work[:, start + j : start + j + 1], (rows, width)) for j in range(STRIP)]
        for k in range(STRIP):
            root = lax.rsqrt(column[k][k : k + 1, :])
            pivot_row = work[k : k + 1, :] * root
            below = jnp.where(row > k, column[k] * root, 0.0)
            work = jnp.where(row == k, pivot_row, work - below * pivot_row)
            for j in range(k + 1, STRIP):
                column[j] = column[j] - below * (column[j][k : k + 1, :] * root)
        done.append(work[:STRIP])
        work = work[STRIP:]
    return jnp.concatenate(done, 0)


def invert_kernel(place_ref, mine_ref, other_ref, out_ref, work, lower):
    core, part = place_ref[CORE], mine_ref.shape[0]
    lower[pl.ds(pl.multiple_of(core * part, part), part), :] = mine_ref[...]
    lower[pl.ds(pl.multiple_of((1 - core) * part, part), part), :] = other_ref[...]
    work[:, :HALF] = lower[:PANEL, :]
    work[:HALF, HALF:PANEL] = lower[HALF:PANEL, :].T
    work[HALF:, HALF:PANEL] = lower[PANEL:, :]
    row = lax.broadcasted_iota(jnp.int32, (PANEL, PANEL), 0)
    col = lax.broadcasted_iota(jnp.int32, (PANEL, PANEL), 1)
    work[:, PANEL:] = jnp.where(row == col, 1.0, 0.0).astype(F32)
    row = lax.broadcasted_iota(jnp.int32, (BLOCK, 128), 0)
    col = lax.broadcasted_iota(jnp.int32, (BLOCK, 128), 1)
    for low in range(0, PANEL, BLOCK):
        base = low // 128 * 128
        square = work[low : low + BLOCK, base : base + 128]
        if low > base:
            square = pltpu.roll(square, 128 - (low - base), 1)
        square = jnp.where(col < BLOCK, square, jnp.where(col - BLOCK == row, 1.0, 0.0))
        corner = pltpu.roll(eliminate(square), 128 - BLOCK, 1)[:, :BLOCK]
        end = PANEL + (low + BLOCK + 127) // 128 * 128
        scaled = jnp.dot(corner, work[low : low + BLOCK, base:end], precision=HIGHEST, preferred_element_type=F32)
        work[low : low + BLOCK, base:end] = scaled
        rest = low + BLOCK
        if rest < PANEL:
            left = rest // 128 * 128
            update = lax.dot_general(
                scaled[:, left - base : PANEL - base],
                scaled[:, left - base :],
                (((0,), (0,)), ((), ())),
                precision=HIGHEST,
                preferred_element_type=F32,
            )
            work[rest:PANEL, left:end] = work[rest:PANEL, left:end] - update[rest - left :]
    row = lax.broadcasted_iota(jnp.int32, (PANEL, PANEL), 0)
    col = lax.broadcasted_iota(jnp.int32, (PANEL, PANEL), 1)
    out_ref[...] = jnp.where(row >= col, work[:, PANEL:], 0.0)


def invert(place, mine, other):
    return pl.pallas_call(
        invert_kernel,
        out_shape=jax.ShapeDtypeStruct((PANEL, PANEL), F32),
        in_specs=[SMEM, VMEM, VMEM],
        out_specs=VMEM,
        scratch_shapes=[pltpu.VMEM((PANEL, 2 * PANEL), F32), pltpu.VMEM((3 * HALF, HALF), F32)],
        compiler_params=PARAMS,
        cost_estimate=pl.CostEstimate(flops=4*10**9, bytes_accessed=2**19, transcendentals=0),
        name="invert",
    )(place, mine, other)


def weigh(total, at, lower_ref, upper_ref, piece):
    low, up = lower_ref[pl.ds(at, 1), :], upper_ref[pl.ds(at, 1), :]
    scaled = (1.0 / (low * low) + 1.0 / (up * up)) / total
    return (piece.astype(F32).T * scaled).astype(jnp.bfloat16)


def piece_at(place_ref, offset, columns):
    return lax.rem(place_ref[AT] + (offset + columns), columns)


def block_lanes(place_ref, block, share):
    return pl.ds(pl.multiple_of(place_ref[BLOCKS + block] * share, share), share)


def fetches(place_ref, basis_ref, columns, offsets, tiles, sems):
    depth = basis_ref.shape[0] // columns
    copies = []
    for i, (offset, tile) in enumerate(zip(offsets, tiles)):
        rows = pl.ds(pl.multiple_of(piece_at(place_ref, offset, columns) * depth, depth), depth)
        copies.append(pltpu.make_async_copy(basis_ref.at[rows, :], tile, sems.at[i]))
    return copies


def gram_kernel(offsets, later, total, fresh, place_ref, lower_ref, upper_ref, basis_ref, *refs):
    number, columns = len(offsets), lower_ref.shape[0]
    pieces, weighted, sems = refs[:number], refs[-number - 1 : -1], refs[-1]
    if fresh:
        outs, tiles = refs[number : -2 * number - 1], refs[-2 * number - 1 : -number - 1]
    else:
        tiles, adds, outs = refs[number : 2 * number], refs[2 * number :], refs[2 * number + 2 : -number - 1]
    copies = fetches(place_ref, basis_ref, columns, later, outs[2:], sems)
    own = fetches(place_ref, basis_ref, columns, offsets, tiles, sems.at[pl.ds(len(later), number)]) if fresh else []
    for copy in own + copies:
        copy.start()
    diagonal = jnp.zeros((PANEL, PANEL), F32) if fresh else adds[1][...]
    for offset, piece, held in zip(offsets, pieces, weighted):
        at = piece_at(place_ref, offset, columns)
        held[...] = weigh(total, at, lower_ref, upper_ref, piece[...])
        diagonal += jnp.dot(held[...], piece[...], preferred_element_type=F32)
    outs[1][...] = diagonal
    for copy in own:
        copy.wait()
    count, _, share = outs[0].shape

    def block(j, carry):
        lanes = block_lanes(place_ref, j, share)
        gram = jnp.zeros((PANEL, share), F32) if fresh else adds[0][j]
        for held, tile in zip(weighted, tiles):
            gram += jnp.dot(held[...], tile[:, lanes], preferred_element_type=F32)
        outs[0][j] = gram
        return carry

    lax.fori_loop(0, count, block, 0)
    for copy in copies:
        copy.wait()


def add_gram(total, shares, shared, sums, pieces, offsets, tiles, later):
    basis, number, depth = shared[-1], len(pieces), pieces[0].shape[0]
    cols = basis.shape[1]
    share = cols // shares
    tile = (depth, cols)
    base = len(shared) + 2 * number
    return pl.pallas_call(
        functools.partial(gram_kernel, offsets, later, float(total), not sums),
        out_shape=[
            jax.ShapeDtypeStruct((shares, PANEL, share), F32),
            jax.ShapeDtypeStruct((PANEL, PANEL), F32),
            *[jax.ShapeDtypeStruct(tile, jnp.bfloat16)] * len(later),
        ],
        in_specs=[SMEM, VMEM, VMEM, HBM] + [VMEM] * (number + len(tiles) + len(sums)),
        out_specs=[VMEM] * (2 + len(later)),
        scratch_shapes=[pltpu.VMEM(tile, jnp.bfloat16)] * (0 if sums else number)
        + [pltpu.VMEM((PANEL, depth), jnp.bfloat16)] * number
        + [pltpu.SemaphoreType.DMA((number + len(later),))],
        compiler_params=PARAMS,
        input_output_aliases={base: 0, base + 1: 1} if sums else {},
        cost_estimate=pl.CostEstimate(
            flops=2 * number * depth * PANEL * cols,
            bytes_accessed=number * depth * cols * 2 + 8 * PANEL * cols,
            transcendentals=0,
        ),
        name="gram",
    )(*shared, *pieces, *tiles, *sums)


def last_kernel(offset, total, place_ref, lower_ref, upper_ref, tile_ref, top_ref, bottom_ref, *refs):
    gram_ref, diagonal_ref, sent_ref, away_ref, mine_ref, other_ref, weighted_ref, sum_ref = refs
    piece = jnp.concatenate([top_ref[...], bottom_ref[...]], 0)
    at = piece_at(place_ref, offset, lower_ref.shape[0])
    weighted_ref[...] = weigh(total, at, lower_ref, upper_ref, piece)
    diagonal = diagonal_ref[...] + jnp.dot(weighted_ref[...], piece, preferred_element_type=F32)
    diagonal = 0.5 * (diagonal + diagonal.T)
    sum_ref[:PANEL, :] = diagonal[:, :HALF]
    sum_ref[PANEL:, :] = diagonal[HALF:, HALF:]
    core, part = place_ref[CORE], mine_ref.shape[0]
    mine_ref[...] = sum_ref[pl.ds(pl.multiple_of(core * part, part), part), :]
    other_ref[...] = sum_ref[pl.ds(pl.multiple_of((1 - core) * part, part), part), :]
    add_blocks(place_ref, gram_ref, weighted_ref, tile_ref, [(3, sent_ref), (1, away_ref)])


def add_blocks(place_ref, gram_ref, weighted_ref, tile_ref, quarters):
    for number, out_ref in quarters:
        count, _, share = out_ref.shape
        for j in range(count):
            block = number * count + j
            lanes = block_lanes(place_ref, block, share)
            term = jnp.dot(weighted_ref[...], tile_ref[:, lanes], preferred_element_type=F32)
            out_ref[j] = gram_ref[block] + term


def rest_kernel(place_ref, weighted_ref, tile_ref, gram_ref, sent_ref, kept_ref):
    add_blocks(place_ref, gram_ref, weighted_ref, tile_ref, [(2, sent_ref), (0, kept_ref)])


def finish_gram(total, shared, sums, tile, top, bottom, offset):
    place, lower, upper, _ = shared
    gram, diagonal = sums
    shares, _, share = gram.shape
    depth = tile.shape[0]
    quarter = jax.ShapeDtypeStruct((shares // 4, PANEL, share), F32)
    half = jax.ShapeDtypeStruct((3 * HALF // 2, HALF), F32)
    cost = pl.CostEstimate(flops=depth * PANEL * share * shares, bytes_accessed=2**21, transcendentals=0)
    third, first, mine, other, weighted = pl.pallas_call(
        functools.partial(last_kernel, offset, float(total)),
        out_shape=[quarter, quarter, half, half, jax.ShapeDtypeStruct((PANEL, depth), jnp.bfloat16)],
        in_specs=[SMEM] + [VMEM] * 7,
        out_specs=[VMEM] * 5,
        scratch_shapes=[pltpu.VMEM((3 * HALF, HALF), F32)],
        compiler_params=PARAMS,
        cost_estimate=cost,
        name="last",
    )(place, lower, upper, tile, top, bottom, gram, diagonal)
    second, zeroth = pl.pallas_call(
        rest_kernel,
        out_shape=[quarter, quarter],
        in_specs=[SMEM] + [VMEM] * 3,
        out_specs=[VMEM] * 2,
        compiler_params=PARAMS,
        cost_estimate=cost,
        name="rest",
    )(place, weighted, tile, gram)
    return zeroth, first, second, third, mine, other


def transform_kernel(inverse_ref, *refs):
    gram = refs[0][0]
    for ref in refs[1:-1]:
        gram = gram + ref[0]
    refs[-1][...] = lax.dot_general(
        gram.T, inverse_ref[...], (((1,), (1,)), ((), ())), precision=HIGHEST, preferred_element_type=F32
    )


def transform(inverse, terms):
    share = terms[0].shape[2]
    return pl.pallas_call(
        transform_kernel,
        out_shape=jax.ShapeDtypeStruct((share, PANEL), F32),
        in_specs=[VMEM] * (1 + len(terms)),
        out_specs=VMEM,
        compiler_params=PARAMS,
        cost_estimate=pl.CostEstimate(
            flops=12 * share * PANEL * PANEL, bytes_accessed=12 * share * PANEL, transcendentals=0
        ),
        name="transform",
    )(inverse, *terms)


def on_device(basis, lower_slack, upper_slack):
    rows = basis.shape[0]
    shares, columns = lax.axis_size("rxn"), lax.axis_size("col")
    me, column = lax.axis_index("rxn"), lax.axis_index("col")
    order = ring_order(columns)
    relay, middle = order[-1], columns // 2
    at = sum(jnp.where(column == c, p, 0) for p, c in enumerate(order))
    blocks = [me ^ reverse_bits(j, shares) for j in range(shares)]
    place = jnp.stack([column, me % 2, at, *blocks]).astype(jnp.int32)
    basis = pltpu.with_memory_space_constraint(basis, pltpu.HBM)
    slacks = [x.reshape(columns, rows // columns) for x in (lower_slack, upper_slack)]
    shared = (place, *slacks, basis)

    near, far = range(1, middle), range(middle + 1, columns)
    choices = [(0, 0), (middle, middle)]
    for pair in zip(near, far):
        choices += [pair, pair[::-1]]
    first, alone, *pieces = cut_panel(place, basis, choices, columns)
    held = first + to_column(alone, [(0, order[middle])])
    for i, (p, q) in enumerate(zip(near, far)):
        came = [
            lax.ppermute(
                pieces[2 * i + k],
                ("rxn", "col"),
                [(r * columns, r * columns + (order[p] if r % 2 == k else relay)) for r in range(shares)],
            )
            for k in range(2)
        ]
        pair = came[0] + came[1]
        if order[q] != relay:
            held = held + to_column(pair, [(relay, order[q])])
            pair = jnp.where(column == relay, 0, pair)
        held = held + pair

    forward = [(order[i], order[(i + 1) % columns]) for i in range(columns)]
    backward = [(b, a) for a, b in forward]
    gram = functools.partial(add_gram, rows * shares, shares, shared)
    pieces, offsets, sums, tiles = [held], [0], [], []
    ahead = back = held
    for step in range(1, middle):
        ahead, back = to_column(ahead, forward), to_column(back, backward)
        later = [-step, step]
        *sums, left, right = gram(sums, pieces, offsets, tiles, later)
        ahead, left, right, *sums = lax.optimization_barrier((ahead, left, right, *sums))
        pieces, offsets, tiles = [ahead, back], later, [left, right]
    cut = rows // columns // 2
    top, bottom = to_column(ahead[:cut], forward), to_column(back[cut:], backward)
    *sums, tile = gram(sums, pieces, offsets, tiles, [middle])
    zeroth, first, second, third, mine, other = finish_gram(rows * shares, shared, sums, tile, top, bottom, middle)

    mine, third = mine + swap(other, 1), swap(third, 1)
    mine, away, second = lax.optimization_barrier((mine, first + third, second))
    part, came, second = swap(mine, 2), swap(away, 2), swap(second, 1)
    mine, bit = mine + part, 4
    while bit < shares:
        mine = mine + swap(mine, bit)
        bit *= 2
    other = swap(mine, 1)
    inverse = invert(place, mine, other)
    terms, bit = [zeroth, second, came], 4
    while bit < shares:
        mine = functools.reduce(lambda a, b: a + b, terms)
        middle = mine.shape[0] // 2
        terms = [mine[:middle], swap(mine[middle:], bit)]
        bit *= 2
    return transform(inverse, terms)


def solution(mesh):
    return jax.shard_map(
        on_device,
        mesh=mesh,
        in_specs=(P("rxn", "col"), P("rxn"), P("rxn")),
        out_specs=P(("col", "rxn"), None),
        check_vma=False,
    )
```

```python
import functools

import jax
import jax.numpy as jnp
from jax import lax
from jax.experimental import pallas as pl
from jax.experimental.pallas import tpu as pltpu
from jax.sharding import PartitionSpec as P

PANEL = 256
HALF = PANEL // 2
LANES = 128
BLOCK = 64
STRIP = 16
COLUMN, CORE, AT, BLOCKS = 0, 1, 2, 3
SMEM, VMEM, HBM = (pl.BlockSpec(memory_space=space) for space in (pltpu.SMEM, pltpu.VMEM, pltpu.HBM))
HIGHEST = lax.Precision.HIGHEST
F32 = jnp.float32
PARAMS = pltpu.CompilerParams(vmem_limit_bytes=16 * 2**20)


def ring_order(columns):
    return list(range(0, columns, 2)) + list(range(columns - 1, 0, -2))


def reverse_bits(value, count):
    out, bit = 0, 1
    while bit < count:
        out = out * 2 + (1 if value & bit else 0)
        bit *= 2
    return out


def to_column(value, pairs):
    return lax.ppermute(value, "col", pairs)


def swap(value, bit, column=None):
    shares, columns = lax.axis_size("rxn"), lax.axis_size("col")
    on = range(columns) if column is None else [column]
    pairs = [(i * columns + c, (i ^ bit) * columns + c) for i in range(shares) for c in on]
    return lax.ppermute(value, ("rxn", "col"), pairs)


def cut_kernel(choices, place_ref, basis_ref, *refs):
    pieces, sems = refs[:-1], refs[-1]
    pieces[0][...] = jnp.zeros_like(pieces[0])

    @pl.when(place_ref[COLUMN] == 0)
    def _():
        depth = pieces[0].shape[0]
        copies = []
        for i, (piece, choice) in enumerate(zip(pieces, choices)):
            row = pl.multiple_of(jnp.where(place_ref[CORE] == 0, choice[0], choice[1]) * depth, depth)
            copies.append(
                pltpu.make_async_copy(basis_ref.at[pl.ds(row, depth), pl.ds(0, PANEL)], piece, sems.at[i])
            )
        for copy in copies:
            copy.start()
        for copy in copies:
            copy.wait()


def cut_panel(place, basis, choices, count):
    depth = basis.shape[0] // count
    return pl.pallas_call(
        functools.partial(cut_kernel, choices),
        out_shape=[jax.ShapeDtypeStruct((depth, PANEL), jnp.bfloat16)] * len(choices),
        in_specs=[SMEM, HBM],
        out_specs=[VMEM] * len(choices),
        scratch_shapes=[pltpu.SemaphoreType.DMA((len(choices),))],
        compiler_params=PARAMS,
        name="cut_panel",
    )(place, basis)


def eliminate(work):
    done, width = [], work.shape[1]
    for start in range(0, work.shape[0], STRIP):
        rows = work.shape[0]
        row = lax.broadcasted_iota(jnp.int32, (rows, width), 0)
        column = [jnp.broadcast_to(work[:, start + j : start + j + 1], (rows, width)) for j in range(STRIP)]
        for k in range(STRIP):
            root = lax.rsqrt(column[k][k : k + 1, :])
            pivot_row = work[k : k + 1, :] * root
            below = jnp.where(row > k, column[k] * root, 0.0)
            work = jnp.where(row == k, pivot_row, work - below * pivot_row)
            for j in range(k + 1, STRIP):
                column[j] = column[j] - below * (column[j][k : k + 1, :] * root)
        done.append(work[:STRIP])
        work = work[STRIP:]
    return jnp.concatenate(done, 0)


def invert_kernel(place_ref, mine_ref, other_ref, out_ref, work, lower):
    core, part = place_ref[CORE], mine_ref.shape[0]
    lower[pl.ds(pl.multiple_of(core * part, part), part), :] = mine_ref[...]
    lower[pl.ds(pl.multiple_of((1 - core) * part, part), part), :] = other_ref[...]
    work[:, :HALF] = lower[:PANEL, :]
    work[:HALF, HALF:PANEL] = lower[HALF:PANEL, :].T
    work[HALF:, HALF:PANEL] = lower[PANEL:, :]
    row = lax.broadcasted_iota(jnp.int32, (PANEL, PANEL), 0)
    col = lax.broadcasted_iota(jnp.int32, (PANEL, PANEL), 1)
    work[:, PANEL:] = jnp.where(row == col, 1.0, 0.0).astype(F32)
    row = lax.broadcasted_iota(jnp.int32, (BLOCK, 128), 0)
    col = lax.broadcasted_iota(jnp.int32, (BLOCK, 128), 1)
    for low in range(0, PANEL, BLOCK):
        base = low // 128 * 128
        square = work[low : low + BLOCK, base : base + 128]
        if low > base:
            square = pltpu.roll(square, 128 - (low - base), 1)
        square = jnp.where(col < BLOCK, square, jnp.where(col - BLOCK == row, 1.0, 0.0))
        corner = pltpu.roll(eliminate(square), 128 - BLOCK, 1)[:, :BLOCK]
        end = PANEL + (low + BLOCK + 127) // 128 * 128
        scaled = jnp.dot(corner, work[low : low + BLOCK, base:end], precision=HIGHEST, preferred_element_type=F32)
        work[low : low + BLOCK, base:end] = scaled
        rest = low + BLOCK
        if rest < PANEL:
            left = rest // 128 * 128
            update = lax.dot_general(
                scaled[:, left - base : PANEL - base],
                scaled[:, left - base :],
                (((0,), (0,)), ((), ())),
                precision=HIGHEST,
                preferred_element_type=F32,
            )
            work[rest:PANEL, left:end] = work[rest:PANEL, left:end] - update[rest - left :]
    row = lax.broadcasted_iota(jnp.int32, (PANEL, PANEL), 0)
    col = lax.broadcasted_iota(jnp.int32, (PANEL, PANEL), 1)
    out_ref[...] = jnp.where(row >= col, work[:, PANEL:], 0.0)


def invert(place, mine, other):
    return pl.pallas_call(
        invert_kernel,
        out_shape=jax.ShapeDtypeStruct((PANEL, PANEL), F32),
        in_specs=[SMEM, VMEM, VMEM],
        out_specs=VMEM,
        scratch_shapes=[pltpu.VMEM((PANEL, 2 * PANEL), F32), pltpu.VMEM((3 * HALF, HALF), F32)],
        compiler_params=PARAMS,
        cost_estimate=pl.CostEstimate(flops=10*10**8, bytes_accessed=2**19, transcendentals=0),
        name="invert",
    )(place, mine, other)


def weigh(total, at, lower_ref, upper_ref, piece):
    low, up = lower_ref[pl.ds(at, 1), :], upper_ref[pl.ds(at, 1), :]
    scaled = (1.0 / (low * low) + 1.0 / (up * up)) / total
    return (piece.astype(F32).T * scaled).astype(jnp.bfloat16)


def piece_at(place_ref, offset, columns):
    return lax.rem(place_ref[AT] + (offset + columns), columns)


def block_lanes(place_ref, block, share):
    return pl.ds(pl.multiple_of(place_ref[BLOCKS + block] * share, share), share)


def fetches(place_ref, basis_ref, columns, offsets, tiles, sems):
    depth = basis_ref.shape[0] // columns
    copies = []
    for i, (offset, tile) in enumerate(zip(offsets, tiles)):
        rows = pl.ds(pl.multiple_of(piece_at(place_ref, offset, columns) * depth, depth), depth)
        copies.append(pltpu.make_async_copy(basis_ref.at[rows, :], tile, sems.at[i]))
    return copies


def gram_kernel(offsets, later, total, fresh, place_ref, lower_ref, upper_ref, basis_ref, *refs):
    number, columns = len(offsets), lower_ref.shape[0]
    pieces, weighted, sems = refs[:number], refs[-number - 1 : -1], refs[-1]
    if fresh:
        outs, tiles = refs[number : -2 * number - 1], refs[-2 * number - 1 : -number - 1]
    else:
        tiles, adds, outs = refs[number : 2 * number], refs[2 * number :], refs[2 * number + 2 : -number - 1]
    copies = fetches(place_ref, basis_ref, columns, later, outs[2:], sems)
    own = fetches(place_ref, basis_ref, columns, offsets, tiles, sems.at[pl.ds(len(later), number)]) if fresh else []
    for copy in own + copies:
        copy.start()
    diagonal = jnp.zeros((PANEL, PANEL), F32) if fresh else adds[1][...]
    for offset, piece, held in zip(offsets, pieces, weighted):
        at = piece_at(place_ref, offset, columns)
        held[...] = weigh(total, at, lower_ref, upper_ref, piece[...])
        diagonal += jnp.dot(held[...], piece[...], preferred_element_type=F32)
    outs[1][...] = diagonal
    for copy in own:
        copy.wait()
    count, _, share = outs[0].shape

    def block(j, carry):
        lanes = block_lanes(place_ref, j, share)
        gram = jnp.zeros((PANEL, share), F32) if fresh else adds[0][j]
        for held, tile in zip(weighted, tiles):
            gram += jnp.dot(held[...], tile[:, lanes], preferred_element_type=F32)
        outs[0][j] = gram
        return carry

    lax.fori_loop(0, count, block, 0)
    for copy in copies:
        copy.wait()


def add_gram(total, shares, shared, sums, pieces, offsets, tiles, later):
    basis, number, depth = shared[-1], len(pieces), pieces[0].shape[0]
    cols = basis.shape[1]
    share = cols // shares
    tile = (depth, cols)
    base = len(shared) + 2 * number
    return pl.pallas_call(
        functools.partial(gram_kernel, offsets, later, float(total), not sums),
        out_shape=[
            jax.ShapeDtypeStruct((shares, PANEL, share), F32),
            jax.ShapeDtypeStruct((PANEL, PANEL), F32),
            *[jax.ShapeDtypeStruct(tile, jnp.bfloat16)] * len(later),
        ],
        in_specs=[SMEM, VMEM, VMEM, HBM] + [VMEM] * (number + len(tiles) + len(sums)),
        out_specs=[VMEM] * (2 + len(later)),
        scratch_shapes=[pltpu.VMEM(tile, jnp.bfloat16)] * (0 if sums else number)
        + [pltpu.VMEM((PANEL, depth), jnp.bfloat16)] * number
        + [pltpu.SemaphoreType.DMA((number + len(later),))],
        compiler_params=PARAMS,
        input_output_aliases={base: 0, base + 1: 1} if sums else {},
        cost_estimate=pl.CostEstimate(
            flops=2 * number * depth * PANEL * cols,
            bytes_accessed=number * depth * cols * 2 + 8 * PANEL * cols,
            transcendentals=0,
        ),
        name="gram",
    )(*shared, *pieces, *tiles, *sums)


def last_kernel(offset, total, place_ref, lower_ref, upper_ref, tile_ref, top_ref, bottom_ref, *refs):
    gram_ref, diagonal_ref, *outs, mine_ref, other_ref, weighted_ref, sum_ref = refs
    piece = jnp.concatenate([top_ref[...], bottom_ref[...]], 0)
    at = piece_at(place_ref, offset, lower_ref.shape[0])
    weighted_ref[...] = weigh(total, at, lower_ref, upper_ref, piece)
    diagonal = diagonal_ref[...] + jnp.dot(weighted_ref[...], piece, preferred_element_type=F32)
    diagonal = 0.5 * (diagonal + diagonal.T)
    sum_ref[:PANEL, :] = diagonal[:, :HALF]
    sum_ref[PANEL:, :] = diagonal[HALF:, HALF:]
    core, part = place_ref[CORE], mine_ref.shape[0]
    mine_ref[...] = sum_ref[pl.ds(pl.multiple_of(core * part, part), part), :]
    other_ref[...] = sum_ref[pl.ds(pl.multiple_of((1 - core) * part, part), part), :]
    add_blocks(place_ref, gram_ref, weighted_ref, tile_ref, [(3, outs[:2]), (1, outs[2:])])


def add_blocks(place_ref, gram_ref, weighted_ref, tile_ref, quarters):
    for number, outs in quarters:
        count, height, share = outs[0].shape
        for j in range(count):
            block = number * count + j
            lanes = block_lanes(place_ref, block, share)
            gram = gram_ref[block] + jnp.dot(weighted_ref[...], tile_ref[:, lanes], preferred_element_type=F32)
            for i, out_ref in enumerate(outs):
                out_ref[j] = gram[i * height : (i + 1) * height]


def rest_kernel(place_ref, weighted_ref, tile_ref, gram_ref, sent_ref, kept_ref):
    add_blocks(place_ref, gram_ref, weighted_ref, tile_ref, [(2, [sent_ref]), (0, [kept_ref])])


def finish_gram(total, shared, sums, tile, top, bottom, offset):
    place, lower, upper, _ = shared
    gram, diagonal = sums
    shares, _, share = gram.shape
    depth = tile.shape[0]
    quarter = jax.ShapeDtypeStruct((shares // 4, PANEL, share), F32)
    eighth = jax.ShapeDtypeStruct((shares // 4, HALF, share), F32)
    half = jax.ShapeDtypeStruct((3 * HALF // 2, HALF), F32)
    cost = pl.CostEstimate(flops=depth * PANEL * share * shares, bytes_accessed=2**21, transcendentals=0)
    *thirds, first, other_first, mine, other, weighted = pl.pallas_call(
        functools.partial(last_kernel, offset, float(total)),
        out_shape=[eighth] * 4 + [half, half, jax.ShapeDtypeStruct((PANEL, depth), jnp.bfloat16)],
        in_specs=[SMEM] + [VMEM] * 7,
        out_specs=[VMEM] * 7,
        scratch_shapes=[pltpu.VMEM((3 * HALF, HALF), F32)],
        compiler_params=PARAMS,
        cost_estimate=cost,
        name="last",
    )(place, lower, upper, tile, top, bottom, gram, diagonal)
    second, zeroth = pl.pallas_call(
        rest_kernel,
        out_shape=[quarter, quarter],
        in_specs=[SMEM] + [VMEM] * 3,
        out_specs=[VMEM] * 2,
        compiler_params=PARAMS,
        cost_estimate=cost,
        name="rest",
    )(place, weighted, tile, gram)
    return zeroth, (first, other_first), second, thirds, mine, other


def transform_kernel(part, inverse_ref, *refs):
    *terms, out_ref = refs
    rows = slice(part * HALF, (part + 1) * HALF)
    grams = [ref[0, rows, :] if ref.shape[1] == PANEL else ref[0] for ref in terms[part:]]
    gram = functools.reduce(lambda a, b: a + b, grams).T
    product = lax.dot_general(
        gram,
        inverse_ref[part * HALF :, rows],
        (((1,), (1,)), ((), ())),
        precision=HIGHEST,
        preferred_element_type=F32,
    )
    if part:
        out_ref[:, :HALF] = terms[0][:, :HALF]
        out_ref[:, HALF:] = terms[0][:, HALF:] + product
    else:
        out_ref[...] = product


def transform(part, inverse, terms):
    share = terms[-1].shape[2]
    return pl.pallas_call(
        functools.partial(transform_kernel, part),
        out_shape=jax.ShapeDtypeStruct((share, PANEL), F32),
        in_specs=[VMEM] * (1 + len(terms)),
        out_specs=VMEM,
        compiler_params=PARAMS,
        cost_estimate=pl.CostEstimate(
            flops=6 * share * PANEL * PANEL, bytes_accessed=8 * share * PANEL, transcendentals=0
        ),
        name="transform",
    )(inverse, *terms)


def on_device(basis, lower_slack, upper_slack):
    rows = basis.shape[0]
    shares, columns = lax.axis_size("rxn"), lax.axis_size("col")
    me, column = lax.axis_index("rxn"), lax.axis_index("col")
    order = ring_order(columns)
    relay, middle = order[-1], columns // 2
    at = sum(jnp.where(column == c, p, 0) for p, c in enumerate(order))
    blocks = [me ^ reverse_bits(j, shares) for j in range(shares)]
    place = jnp.stack([column, me % 2, at, *blocks]).astype(jnp.int32)
    basis = pltpu.with_memory_space_constraint(basis, pltpu.HBM)
    slacks = [x.reshape(columns, rows // columns) for x in (lower_slack, upper_slack)]
    shared = (place, *slacks, basis)

    near, far = range(1, middle), range(middle + 1, columns)
    choices = [(0, 0), (middle, middle)]
    for pair in zip(near, far):
        choices += [pair, pair[::-1]]
    first, alone, *pieces = cut_panel(place, basis, choices, columns)
    held = first + to_column(alone, [(0, order[middle])])
    for i, (p, q) in enumerate(zip(near, far)):
        came = [
            lax.ppermute(
                pieces[2 * i + k],
                ("rxn", "col"),
                [(r * columns, r * columns + (order[p] if r % 2 == k else relay)) for r in range(shares)],
            )
            for k in range(2)
        ]
        pair = came[0] + came[1]
        if order[q] != relay:
            held = held + to_column(pair, [(relay, order[q])])
            pair = jnp.where(column == relay, 0, pair)
        held = held + pair

    forward = [(order[i], order[(i + 1) % columns]) for i in range(columns)]
    backward = [(b, a) for a, b in forward]
    gram = functools.partial(add_gram, rows * shares, shares, shared)
    pieces, offsets, sums, tiles = [held], [0], [], []
    ahead = back = held
    for step in range(1, middle):
        ahead, back = to_column(ahead, forward), to_column(back, backward)
        later = [-step, step]
        *sums, left, right = gram(sums, pieces, offsets, tiles, later)
        back, left, right, *sums = lax.optimization_barrier((back, left, right, *sums))
        pieces, offsets, tiles = [ahead, back], later, [left, right]
    cut = rows // columns // 2
    top, bottom = to_column(ahead[:cut], forward), to_column(back[cut:], backward)
    *sums, tile = gram(sums, pieces, offsets, tiles, [middle])
    zeroth, first, second, thirds, mine, other = finish_gram(rows * shares, shared, sums, tile, top, bottom, middle)

    mine = mine + swap(other, 1)
    away = [x + swap(y, 1) for x, y in zip(first, thirds)]
    mine, second = lax.optimization_barrier((mine, second))
    part, came, second = swap(mine, 2), [swap(x, 2) for x in away], swap(second, 1)
    mine, bit = mine + part, 4
    while bit < shares:
        mine = mine + swap(mine, bit)
        bit *= 2
    inverse = invert(place, mine, swap(mine, 1))
    out = []
    for i in range(2):
        terms, bit = [zeroth, second, came[i]], 4
        while bit < shares:
            lane = slice(i * HALF, (i + 1) * HALF)
            mine = sum(x[:, lane] if x.shape[1] == PANEL else x for x in terms)
            half = mine.shape[0] // 2
            terms = [mine[:half], swap(mine[half:], bit)]
            bit *= 2
        out = transform(i, inverse, [out, *terms] if i else terms)
    return out


def solution(mesh):
    return jax.shard_map(
        on_device,
        mesh=mesh,
        in_specs=(P("rxn", "col"), P("rxn"), P("rxn")),
        out_specs=P(("col", "rxn"), None),
        check_vma=False,
    )
```

```python
import functools

import jax
import jax.numpy as jnp
from jax import lax
from jax.experimental import pallas as pl
from jax.experimental.pallas import tpu as pltpu
from jax.sharding import PartitionSpec as P

PANEL = 256
HALF = PANEL // 2
LANES = 128
BLOCK = 64
STRIP = 16
COLUMN, CORE, AT, BLOCKS = 0, 1, 2, 3
SMEM, VMEM, HBM = (pl.BlockSpec(memory_space=space) for space in (pltpu.SMEM, pltpu.VMEM, pltpu.HBM))
HIGHEST = lax.Precision.HIGHEST
F32 = jnp.float32
PARAMS = pltpu.CompilerParams(vmem_limit_bytes=16 * 2**20)


def ring_order(columns):
    return list(range(0, columns, 2)) + list(range(columns - 1, 0, -2))


def reverse_bits(value, count):
    out, bit = 0, 1
    while bit < count:
        out = out * 2 + (1 if value & bit else 0)
        bit *= 2
    return out


def to_column(value, pairs):
    return lax.ppermute(value, "col", pairs)


def swap(value, bit, column=None):
    shares, columns = lax.axis_size("rxn"), lax.axis_size("col")
    on = range(columns) if column is None else [column]
    pairs = [(i * columns + c, (i ^ bit) * columns + c) for i in range(shares) for c in on]
    return lax.ppermute(value, ("rxn", "col"), pairs)


def cut_kernel(choices, place_ref, basis_ref, *refs):
    pieces, sems = refs[:-1], refs[-1]
    pieces[0][...] = jnp.zeros_like(pieces[0])

    @pl.when(place_ref[COLUMN] == 0)
    def _():
        depth = pieces[0].shape[0]
        copies = []
        for i, (piece, choice) in enumerate(zip(pieces, choices)):
            row = pl.multiple_of(jnp.where(place_ref[CORE] == 0, choice[0], choice[1]) * depth, depth)
            copies.append(
                pltpu.make_async_copy(basis_ref.at[pl.ds(row, depth), pl.ds(0, PANEL)], piece, sems.at[i])
            )
        for copy in copies:
            copy.start()
        for copy in copies:
            copy.wait()


def cut_panel(place, basis, choices, count):
    depth = basis.shape[0] // count
    return pl.pallas_call(
        functools.partial(cut_kernel, choices),
        out_shape=[jax.ShapeDtypeStruct((depth, PANEL), jnp.bfloat16)] * len(choices),
        in_specs=[SMEM, HBM],
        out_specs=[VMEM] * len(choices),
        scratch_shapes=[pltpu.SemaphoreType.DMA((len(choices),))],
        compiler_params=PARAMS,
        name="cut_panel",
    )(place, basis)


def eliminate(work):
    done, width = [], work.shape[1]
    for start in range(0, work.shape[0], STRIP):
        rows = work.shape[0]
        row = lax.broadcasted_iota(jnp.int32, (rows, width), 0)
        column = [jnp.broadcast_to(work[:, start + j : start + j + 1], (rows, width)) for j in range(STRIP)]
        for k in range(STRIP):
            root = lax.rsqrt(column[k][k : k + 1, :])
            pivot_row = work[k : k + 1, :] * root
            below = jnp.where(row > k, column[k] * root, 0.0)
            work = jnp.where(row == k, pivot_row, work - below * pivot_row)
            for j in range(k + 1, STRIP):
                column[j] = column[j] - below * (column[j][k : k + 1, :] * root)
        done.append(work[:STRIP])
        work = work[STRIP:]
    return jnp.concatenate(done, 0)


def invert_kernel(place_ref, mine_ref, other_ref, out_ref, work, lower):
    core, part = place_ref[CORE], mine_ref.shape[0]
    lower[pl.ds(pl.multiple_of(core * part, part), part), :] = mine_ref[...]
    lower[pl.ds(pl.multiple_of((1 - core) * part, part), part), :] = other_ref[...]
    work[:, :HALF] = lower[:PANEL, :]
    work[:HALF, HALF:PANEL] = lower[HALF:PANEL, :].T
    work[HALF:, HALF:PANEL] = lower[PANEL:, :]
    row = lax.broadcasted_iota(jnp.int32, (PANEL, PANEL), 0)
    col = lax.broadcasted_iota(jnp.int32, (PANEL, PANEL), 1)
    work[:, PANEL:] = jnp.where(row == col, 1.0, 0.0).astype(F32)
    row = lax.broadcasted_iota(jnp.int32, (BLOCK, 128), 0)
    col = lax.broadcasted_iota(jnp.int32, (BLOCK, 128), 1)
    for low in range(0, PANEL, BLOCK):
        base = low // 128 * 128
        square = work[low : low + BLOCK, base : base + 128]
        if low > base:
            square = pltpu.roll(square, 128 - (low - base), 1)
        square = jnp.where(col < BLOCK, square, jnp.where(col - BLOCK == row, 1.0, 0.0))
        corner = pltpu.roll(eliminate(square), 128 - BLOCK, 1)[:, :BLOCK]
        end = PANEL + (low + BLOCK + 127) // 128 * 128
        scaled = jnp.dot(corner, work[low : low + BLOCK, base:end], precision=HIGHEST, preferred_element_type=F32)
        work[low : low + BLOCK, base:end] = scaled
        rest = low + BLOCK
        if rest < PANEL:
            left = rest // 128 * 128
            update = lax.dot_general(
                scaled[:, left - base : PANEL - base],
                scaled[:, left - base :],
                (((0,), (0,)), ((), ())),
                precision=HIGHEST,
                preferred_element_type=F32,
            )
            work[rest:PANEL, left:end] = work[rest:PANEL, left:end] - update[rest - left :]
    row = lax.broadcasted_iota(jnp.int32, (PANEL, PANEL), 0)
    col = lax.broadcasted_iota(jnp.int32, (PANEL, PANEL), 1)
    out_ref[...] = jnp.where(row >= col, work[:, PANEL:], 0.0)


def invert(place, mine, other):
    return pl.pallas_call(
        invert_kernel,
        out_shape=jax.ShapeDtypeStruct((PANEL, PANEL), F32),
        in_specs=[SMEM, VMEM, VMEM],
        out_specs=VMEM,
        scratch_shapes=[pltpu.VMEM((PANEL, 2 * PANEL), F32), pltpu.VMEM((3 * HALF, HALF), F32)],
        compiler_params=PARAMS,
        cost_estimate=pl.CostEstimate(flops=10*10**8, bytes_accessed=2**19, transcendentals=0),
        name="invert",
    )(place, mine, other)


def weigh(total, at, lower_ref, upper_ref, piece):
    low, up = lower_ref[pl.ds(at, 1), :], upper_ref[pl.ds(at, 1), :]
    scaled = (1.0 / (low * low) + 1.0 / (up * up)) / total
    return (piece.astype(F32).T * scaled).astype(jnp.bfloat16)


def piece_at(place_ref, offset, columns):
    return lax.rem(place_ref[AT] + (offset + columns), columns)


def block_lanes(place_ref, block, share):
    return pl.ds(pl.multiple_of(place_ref[BLOCKS + block] * share, share), share)


def fetches(place_ref, basis_ref, columns, offsets, tiles, sems):
    depth = basis_ref.shape[0] // columns
    copies = []
    for i, (offset, tile) in enumerate(zip(offsets, tiles)):
        rows = pl.ds(pl.multiple_of(piece_at(place_ref, offset, columns) * depth, depth), depth)
        copies.append(pltpu.make_async_copy(basis_ref.at[rows, :], tile, sems.at[i]))
    return copies


def gram_kernel(offsets, later, total, fresh, place_ref, lower_ref, upper_ref, basis_ref, *refs):
    number, columns = len(offsets), lower_ref.shape[0]
    pieces, weighted, sems = refs[:number], refs[-number - 1 : -1], refs[-1]
    if fresh:
        outs, tiles = refs[number : -2 * number - 1], refs[-2 * number - 1 : -number - 1]
    else:
        tiles, adds, outs = refs[number : 2 * number], refs[2 * number :], refs[2 * number + 2 : -number - 1]
    copies = fetches(place_ref, basis_ref, columns, later, outs[2:], sems)
    own = fetches(place_ref, basis_ref, columns, offsets, tiles, sems.at[pl.ds(len(later), number)]) if fresh else []
    for copy in own + copies:
        copy.start()
    diagonal = jnp.zeros((PANEL, PANEL), F32) if fresh else adds[1][...]
    for offset, piece, held in zip(offsets, pieces, weighted):
        at = piece_at(place_ref, offset, columns)
        held[...] = weigh(total, at, lower_ref, upper_ref, piece[...])
        diagonal += jnp.dot(held[...], piece[...], preferred_element_type=F32)
    outs[1][...] = diagonal
    for copy in own:
        copy.wait()
    count, _, share = outs[0].shape

    def block(j, carry):
        lanes = block_lanes(place_ref, j, share)
        gram = jnp.zeros((PANEL, share), F32) if fresh else adds[0][j]
        for held, tile in zip(weighted, tiles):
            gram += jnp.dot(held[...], tile[:, lanes], preferred_element_type=F32)
        outs[0][j] = gram
        return carry

    lax.fori_loop(0, count, block, 0)
    for copy in copies:
        copy.wait()


def add_gram(total, shares, shared, sums, pieces, offsets, tiles, later):
    basis, number, depth = shared[-1], len(pieces), pieces[0].shape[0]
    cols = basis.shape[1]
    share = cols // shares
    tile = (depth, cols)
    base = len(shared) + 2 * number
    return pl.pallas_call(
        functools.partial(gram_kernel, offsets, later, float(total), not sums),
        out_shape=[
            jax.ShapeDtypeStruct((shares, PANEL, share), F32),
            jax.ShapeDtypeStruct((PANEL, PANEL), F32),
            *[jax.ShapeDtypeStruct(tile, jnp.bfloat16)] * len(later),
        ],
        in_specs=[SMEM, VMEM, VMEM, HBM] + [VMEM] * (number + len(tiles) + len(sums)),
        out_specs=[VMEM] * (2 + len(later)),
        scratch_shapes=[pltpu.VMEM(tile, jnp.bfloat16)] * (0 if sums else number)
        + [pltpu.VMEM((PANEL, depth), jnp.bfloat16)] * number
        + [pltpu.SemaphoreType.DMA((number + len(later),))],
        compiler_params=PARAMS,
        input_output_aliases={base: 0, base + 1: 1} if sums else {},
        cost_estimate=pl.CostEstimate(
            flops=2 * number * depth * PANEL * cols,
            bytes_accessed=number * depth * cols * 2 + 8 * PANEL * cols,
            transcendentals=0,
        ),
        name="gram",
    )(*shared, *pieces, *tiles, *sums)


def last_kernel(offset, total, place_ref, lower_ref, upper_ref, tile_ref, top_ref, bottom_ref, *refs):
    gram_ref, diagonal_ref, *outs, mine_ref, other_ref, weighted_ref, sum_ref = refs
    piece = jnp.concatenate([top_ref[...], bottom_ref[...]], 0)
    at = piece_at(place_ref, offset, lower_ref.shape[0])
    weighted_ref[...] = weigh(total, at, lower_ref, upper_ref, piece)
    diagonal = diagonal_ref[...] + jnp.dot(weighted_ref[...], piece, preferred_element_type=F32)
    diagonal = 0.5 * (diagonal + diagonal.T)
    sum_ref[:PANEL, :] = diagonal[:, :HALF]
    sum_ref[PANEL:, :] = diagonal[HALF:, HALF:]
    core, part = place_ref[CORE], mine_ref.shape[0]
    mine_ref[...] = sum_ref[pl.ds(pl.multiple_of(core * part, part), part), :]
    other_ref[...] = sum_ref[pl.ds(pl.multiple_of((1 - core) * part, part), part), :]
    add_blocks(place_ref, gram_ref, weighted_ref, tile_ref, [(3, outs[:2]), (1, outs[2:])])


def add_blocks(place_ref, gram_ref, weighted_ref, tile_ref, quarters):
    for number, outs in quarters:
        count, height, share = outs[0].shape
        for j in range(count):
            block = number * count + j
            lanes = block_lanes(place_ref, block, share)
            gram = gram_ref[block] + jnp.dot(weighted_ref[...], tile_ref[:, lanes], preferred_element_type=F32)
            for i, out_ref in enumerate(outs):
                out_ref[j] = gram[i * height : (i + 1) * height]


def rest_kernel(place_ref, weighted_ref, tile_ref, gram_ref, sent_ref, kept_ref):
    add_blocks(place_ref, gram_ref, weighted_ref, tile_ref, [(2, [sent_ref]), (0, [kept_ref])])


def finish_gram(total, shared, sums, tile, top, bottom, offset):
    place, lower, upper, _ = shared
    gram, diagonal = sums
    shares, _, share = gram.shape
    depth = tile.shape[0]
    quarter = jax.ShapeDtypeStruct((shares // 4, PANEL, share), F32)
    eighth = jax.ShapeDtypeStruct((shares // 4, HALF, share), F32)
    half = jax.ShapeDtypeStruct((3 * HALF // 2, HALF), F32)
    cost = pl.CostEstimate(flops=depth * PANEL * share * shares, bytes_accessed=2**21, transcendentals=0)
    *thirds, first, other_first, mine, other, weighted = pl.pallas_call(
        functools.partial(last_kernel, offset, float(total)),
        out_shape=[eighth] * 4 + [half, half, jax.ShapeDtypeStruct((PANEL, depth), jnp.bfloat16)],
        in_specs=[SMEM] + [VMEM] * 7,
        out_specs=[VMEM] * 7,
        scratch_shapes=[pltpu.VMEM((3 * HALF, HALF), F32)],
        compiler_params=PARAMS,
        cost_estimate=cost,
        name="last",
    )(place, lower, upper, tile, top, bottom, gram, diagonal)
    second, zeroth = pl.pallas_call(
        rest_kernel,
        out_shape=[quarter, quarter],
        in_specs=[SMEM] + [VMEM] * 3,
        out_specs=[VMEM] * 2,
        compiler_params=PARAMS,
        cost_estimate=cost,
        name="rest",
    )(place, weighted, tile, gram)
    return zeroth, (first, other_first), second, thirds, mine, other


def transform_kernel(part, inverse_ref, *refs):
    *terms, out_ref = refs
    rows = slice(part * HALF, (part + 1) * HALF)
    grams = [ref[0, rows, :] if ref.shape[1] == PANEL else ref[0] for ref in terms[part:]]
    gram = functools.reduce(lambda a, b: a + b, grams).T
    product = lax.dot_general(
        gram,
        inverse_ref[part * HALF :, rows],
        (((1,), (1,)), ((), ())),
        precision=HIGHEST,
        preferred_element_type=F32,
    )
    if part:
        out_ref[:, :HALF] = terms[0][:, :HALF]
        out_ref[:, HALF:] = terms[0][:, HALF:] + product
    else:
        out_ref[...] = product


def transform(part, inverse, terms):
    share = terms[-1].shape[2]
    return pl.pallas_call(
        functools.partial(transform_kernel, part),
        out_shape=jax.ShapeDtypeStruct((share, PANEL), F32),
        in_specs=[VMEM] * (1 + len(terms)),
        out_specs=VMEM,
        compiler_params=PARAMS,
        cost_estimate=pl.CostEstimate(
            flops=6 * share * PANEL * PANEL, bytes_accessed=8 * share * PANEL, transcendentals=0
        ),
        name="transform",
    )(inverse, *terms)


def on_device(basis, lower_slack, upper_slack):
    rows = basis.shape[0]
    shares, columns = lax.axis_size("rxn"), lax.axis_size("col")
    me, column = lax.axis_index("rxn"), lax.axis_index("col")
    order = ring_order(columns)
    relay, middle = order[-1], columns // 2
    at = sum(jnp.where(column == c, p, 0) for p, c in enumerate(order))
    blocks = [me ^ reverse_bits(j, shares) for j in range(shares)]
    place = jnp.stack([column, me % 2, at, *blocks]).astype(jnp.int32)
    basis = pltpu.with_memory_space_constraint(basis, pltpu.HBM)
    slacks = [x.reshape(columns, rows // columns) for x in (lower_slack, upper_slack)]
    shared = (place, *slacks, basis)

    near, far = range(1, middle), range(middle + 1, columns)
    choices = [(0, 0), (middle, middle)]
    for pair in zip(near, far):
        choices += [pair, pair[::-1]]
    first, alone, *pieces = cut_panel(place, basis, choices, columns)
    held = first + to_column(alone, [(0, order[middle])])
    for i, (p, q) in enumerate(zip(near, far)):
        came = [
            lax.ppermute(
                pieces[2 * i + k],
                ("rxn", "col"),
                [(r * columns, r * columns + (order[p] if r % 2 == k else relay)) for r in range(shares)],
            )
            for k in range(2)
        ]
        pair = came[0] + came[1]
        if order[q] != relay:
            held = held + to_column(pair, [(relay, order[q])])
            pair = jnp.where(column == relay, 0, pair)
        held = held + pair

    forward = [(order[i], order[(i + 1) % columns]) for i in range(columns)]
    backward = [(b, a) for a, b in forward]
    gram = functools.partial(add_gram, rows * shares, shares, shared)
    pieces, offsets, sums, tiles = [held], [0], [], []
    ahead = back = held
    for step in range(1, middle):
        ahead, back = to_column(ahead, forward), to_column(back, backward)
        later = [-step, step]
        *sums, left, right = gram(sums, pieces, offsets, tiles, later)
        back, left, right, *sums = lax.optimization_barrier((back, left, right, *sums))
        pieces, offsets, tiles = [ahead, back], later, [left, right]
    cut = rows // columns // 2
    top, bottom = to_column(ahead[:cut], forward), to_column(back[cut:], backward)
    *sums, tile = gram(sums, pieces, offsets, tiles, [middle])
    zeroth, first, second, thirds, mine, other = finish_gram(rows * shares, shared, sums, tile, top, bottom, middle)

    mine = mine + swap(other, 1)
    away = [x + swap(y, 1) for x, y in zip(first, thirds)]
    mine, second = lax.optimization_barrier((mine, second))
    part, away_last = swap(mine, 2), away.pop()
    away_last, second = lax.optimization_barrier((away_last, second))
    came, second = [swap(x, 2) for x in (*away, away_last)], swap(second, 1)
    mine, bit = mine + part, 4
    while bit < shares:
        mine = mine + swap(mine, bit)
        bit *= 2
    inverse = invert(place, mine, swap(mine, 1))
    out = []
    for i in range(2):
        terms, bit = [zeroth, second, came[i]], 4
        while bit < shares:
            lane = slice(i * HALF, (i + 1) * HALF)
            mine = sum(x[:, lane] if x.shape[1] == PANEL else x for x in terms)
            half = mine.shape[0] // 2
            terms = [mine[:half], swap(mine[half:], bit)]
            bit *= 2
        out = transform(i, inverse, [out, *terms] if i else terms)
    return out


def solution(mesh):
    return jax.shard_map(
        on_device,
        mesh=mesh,
        in_specs=(P("rxn", "col"), P("rxn"), P("rxn")),
        out_specs=P(("col", "rxn"), None),
        check_vma=False,
    )
```
